32 devices in a mesh: feat: 8 (over z, core), row: 2 (over y), rep: 2 (over x).
Axes of the slice: x: 2, y: 2, z: 4, core: 2. Of those that a mesh axis runs over, the one named last changes fastest.
Arguments:
- activations: bfloat16 [32, 4608], P('feat', ('row', 'rep')), may hold values from -6 to 6
- enc_weight: bfloat16 [4608, 65536], P(('row', 'rep'), 'feat'), may hold values from -0.09375 to 0.09375
- enc_bias: float32 [65536], P('feat'), may hold values from -3 to 3
- dec_weight: bfloat16 [65536, 4608], P('feat', ('row', 'rep')), may hold values from -0.0234375 to 0.0234375
- dec_bias: float32 [4608], P(('row', 'rep')), may hold values from -3 to 3
- first_moment: bfloat16 [65536, 4608], P('feat', ('row', 'rep')), may hold values from -0.059814453 to 0.059814453
- second_moment: bfloat16 [65536, 4608], P('feat', ('row', 'rep')), may hold values from 9.953976e-06 to 0.0009994507
Outputs:
- reconstruction: bfloat16 [32, 4608], P('feat', ('row', 'rep'))
- dec_step: bfloat16 [65536, 4608], P('feat', ('row', 'rep'))
The draws below stay inside these ranges and needn't reach their ends.
All inputs are finite; a program needn't handle non-finite values.
Results may differ from the reference program's by a relative error of at most 0.0053.
Values may be sent and summed in bfloat16 or wider, within the bound.
No kernel may reach another device: no remote copies, remote signals or barrier semaphores. Data moves between devices by JAX's collectives and lax.ppermute only.
A program may use at most 128 MiB of HBM per device.

```python
import math
import jax
import jax.numpy as jnp
from jax import lax

D = 4608
F = 65536
ROWS = 32


def level_of(stream_key, shape, pieces, low, high):
    factor_of, own = 1.0, jax.random.fold_in(stream_key, 6)
    for dim, parts in pieces:
        steps = jnp.exp(jax.random.uniform(jax.random.fold_in(own, dim), (parts,), jnp.float32, low / len(pieces), high / len(pieces)))
        factor_of = factor_of * jnp.repeat(steps, shape[dim] // parts).reshape([-1 if axis == dim else 1 for axis in range(len(shape))])
    return factor_of


def centred(stream_key, dims, spread, bound, cuts=(), dtype=jnp.bfloat16):
    values = jax.random.normal(stream_key, dims, jnp.float32) * spread
    if len(cuts) > 0:
        values = level_of(stream_key, dims, cuts, -0.22, 0.18) * values
    return jnp.clip(values, min=-bound, max=bound).astype(dtype)


def setup_inputs(seed: int = 0) -> dict:
    arg_keys = jax.random.split(jax.random.key(seed), 8)
    return {
        "activations": centred(arg_keys[0], (ROWS, D), 1.0, 6.0, ((0, 8), (1, 4))),
        "enc_weight": centred(arg_keys[1], (D, F), D ** -0.5, 0.09375, ((0, 4), (1, 8))),
        "enc_bias": centred(arg_keys[2], (F,), 0.5, 3.0, ((0, 8),), jnp.float32),
        "dec_weight": centred(arg_keys[3], (F, D), F ** -0.5, 0.0234375, ((0, 8), (1, 4))),
        "dec_bias": centred(arg_keys[4], (D,), 0.5, 3.0, ((0, 4),), jnp.float32),
        "first_moment": centred(arg_keys[5], (F, D), 0.01, 0.059814453, ((0, 8), (1, 4))),
        "second_moment": jnp.clip(jnp.exp(math.log(0.0009994507) - 4.609234 * jax.random.uniform(arg_keys[6], (F, D), jnp.float32) ** level_of(arg_keys[6], (F, D), ((0, 8), (1, 4)), -0.2, 0.2)), 9.953975677490234e-06, 0.0009994507).astype(jnp.bfloat16),
    }


sparsity_coef = 5.0
beta_one = 0.9
beta_two = 0.999
bias_one = 0.99997344
bias_two = 0.095207853
adam_eps = 1e-08
norm_eps = 1e-06

def adam_block(weight, first, second, active_block, count_block, residual):
    wide = weight.astype(jnp.float32)
    row_norm = jnp.sqrt(lax.optimization_barrier(jnp.sum(wide * wide, axis=1)) + norm_eps)
    product = lax.dot_general(active_block, residual, (((0,), (0,)), ((), ())), preferred_element_type=jnp.float32)
    gradient = 2.0 / ROWS * product + sparsity_coef / ROWS * count_block[:, None] * wide / row_norm[:, None]
    moment_one = beta_one * first.astype(jnp.float32) + (1.0 - beta_one) * gradient
    moment_two = beta_two * second.astype(jnp.float32) + (1.0 - beta_two) * gradient * gradient
    return (moment_one / bias_one / (jnp.sqrt(moment_two / bias_two) + adam_eps)).astype(jnp.bfloat16)

def reference(activations, enc_weight, enc_bias, dec_weight, dec_bias, first_moment, second_moment):
    centered = (activations.astype(jnp.float32) - dec_bias).astype(jnp.bfloat16)
    pre_sum = jnp.dot(centered, enc_weight, preferred_element_type=jnp.float32) + enc_bias
    active = jnp.maximum(pre_sum, 0.0).astype(jnp.bfloat16)
    rebuilt = jnp.dot(active, dec_weight, preferred_element_type=jnp.float32) + dec_bias
    residual = (rebuilt - activations.astype(jnp.float32)).astype(jnp.bfloat16)
    counts = lax.optimization_barrier(jnp.sum(active.astype(jnp.float32), axis=0))
    block = math.gcd(F, 4096)
    blocks = F // block
    active_split = active.reshape(ROWS, blocks, block).transpose(1, 0, 2)

    def one_block(items):
        return adam_block(items[0], items[1], items[2], items[3], items[4], residual)
    dec_step = lax.map(one_block, (dec_weight.reshape(blocks, block, D), first_moment.reshape(blocks, block, D), second_moment.reshape(blocks, block, D), active_split, counts.reshape(blocks, block)))
    return (rebuilt.astype(jnp.bfloat16), dec_step.reshape(F, D))
```

```python
import functools

import jax
import jax.experimental.pallas as pl
import jax.experimental.pallas.tpu as pltpu
import jax.numpy as jnp
from jax import lax
from jax.sharding import PartitionSpec as P

sparsity_coef = 5.0
beta_one = 0.9
beta_two = 0.999
bias_one = 0.99997344
bias_two = 0.095207853
adam_eps = 1e-08
norm_eps = 1e-06

f32 = jnp.float32
bf16 = jnp.bfloat16
MIB = 1 << 20
PARTS = ("row", "rep")
VM = pl.BlockSpec(memory_space=pltpu.VMEM)

A = ((1.0 - beta_two) / beta_two) ** 0.5
K = (1.0 - beta_one) / beta_one / A
C = beta_one / bias_one / (beta_two / bias_two) ** 0.5
E = adam_eps * bias_one / beta_one


def params(mib):
    return pltpu.CompilerParams(vmem_limit_bytes=mib * MIB)


def cost(flops, read):
    return pl.CostEstimate(flops=flops, bytes_accessed=read, transcendentals=0)


def swap(x, axis, n, k):
    return lax.ppermute(x, axis, [(a, a ^ k) for a in range(n)])


def place(parts, axis_sizes):
    index = 0
    for name, size in zip(parts, axis_sizes):
        index = index * size + lax.axis_index(name)
    return index


def encode_kernel(me_ref, *refs):
    rows, (bias_ref, w_ref), (rows_ref, *outs) = refs[:4], refs[4:6], refs[6:]
    x = jnp.concatenate([r[...] for r in rows], axis=0)
    rows_ref[...] = x
    centered = (x - bias_ref[...]).astype(bf16)
    chunk = outs[0].shape[1]
    wide = 512
    for k, out in enumerate(outs):
        start = jnp.bitwise_xor(me_ref[0], k) * chunk

        @pl.loop(0, chunk // wide)
        def _(t):
            s = pl.ds(pl.multiple_of(start + t * wide, 128), wide)
            out[:, pl.ds(pl.multiple_of(t * wide, 128), wide)] = jnp.dot(
                centered, w_ref[:, s], preferred_element_type=f32
            ).astype(bf16)


def encode(me, rows, bias, w, parts):
    depth, width = w.shape
    total = sum(r.shape[0] for r in rows)
    out = jax.ShapeDtypeStruct((total, width // parts), bf16)
    return pl.pallas_call(
        encode_kernel,
        in_specs=[pl.BlockSpec(memory_space=pltpu.SMEM)] + [VM] * (len(rows) + 2),
        out_specs=[VM] * (parts + 1),
        out_shape=[jax.ShapeDtypeStruct((total, depth), f32)] + [out] * parts,
        compiler_params=params(6),
        cost_estimate=cost(2 * total * depth * width, 2 * depth * width),
        name="encode",
    )(me, *rows, bias, pltpu.with_memory_space_constraint(w, pltpu.VMEM))


def active_kernel(me_ref, bias_ref, *refs):
    out = refs[-1]
    chunk = out.shape[1]
    total = refs[0][...].astype(f32)
    for r in refs[1:-1]:
        total = total + r[...].astype(f32)
    start = pl.multiple_of(me_ref[0] * chunk, 128)
    out[...] = jnp.maximum(total + bias_ref[:, pl.ds(start, chunk)], 0.0).astype(bf16)


def activate(me, bias, partials):
    return pl.pallas_call(
        active_kernel,
        in_specs=[pl.BlockSpec(memory_space=pltpu.SMEM)] + [VM] * (len(partials) + 1),
        out_specs=VM,
        out_shape=jax.ShapeDtypeStruct(partials[0].shape, bf16),
        compiler_params=params(4),
        name="activate",
    )(me, bias, *partials)


def squares_kernel(w_ref, out_ref):
    tall = 256
    one = jnp.ones((8, w_ref.shape[1]), bf16)

    @pl.loop(0, w_ref.shape[0] // tall)
    def _(t):
        w = w_ref[pl.ds(pl.multiple_of(t * tall, tall), tall), :]
        total = lax.dot_general(one, w * w, (((1,), (1,)), ((), ())), preferred_element_type=f32)
        out_ref[:, pl.ds(pl.multiple_of(t * tall, tall), tall)] = total[:1]


def squares(w):
    return pl.pallas_call(
        squares_kernel,
        in_specs=[VM],
        out_specs=VM,
        out_shape=jax.ShapeDtypeStruct((1, w.shape[0]), f32),
        compiler_params=params(4),
        cost_estimate=cost(16 * w.size, 2 * w.size),
        name="squares",
    )(w)


def rebuild_kernel(me_ref, *refs):
    parts = len(refs) - 3
    acts, w_ref, out_ref, all_ref = refs[:parts], refs[parts], refs[-2], refs[-1]
    chunk = acts[0].shape[1]
    tall = 1024
    total = jnp.zeros(out_ref.shape, f32)
    for k, act in enumerate(acts):
        start = jnp.bitwise_xor(me_ref[0], k) * chunk
        all_ref[:, pl.ds(pl.multiple_of(start, 128), chunk)] = act[...]

        def body(t, acc):
            rows = pl.ds(pl.multiple_of(start + t * tall, 128), tall)
            mine = act[:, pl.ds(pl.multiple_of(t * tall, 128), tall)]
            return acc + jnp.dot(mine, w_ref[rows, :], preferred_element_type=f32)

        total = lax.fori_loop(0, chunk // tall, body, total)
    out_ref[...] = total


def rebuild(me, acts, w):
    total = acts[0].shape[0]
    return pl.pallas_call(
        rebuild_kernel,
        in_specs=[pl.BlockSpec(memory_space=pltpu.SMEM)] + [VM] * (len(acts) + 1),
        out_specs=[VM, VM],
        out_shape=[
            jax.ShapeDtypeStruct((total, w.shape[1]), f32),
            jax.ShapeDtypeStruct((total, w.shape[0]), bf16),
        ],
        compiler_params=params(6),
        cost_estimate=cost(2 * total * w.size, 2 * w.size),
        name="rebuild",
    )(me, *acts, w)


def pair_kernel(mine_ref, other_ref, wide_ref, out_ref):
    groups = mine_ref.shape[0] // 8
    for q in range(groups):
        s = slice(8 * q, 8 * q + 8)
        wide_ref[s, :] = mine_ref[s, :] + pltpu.roll(other_ref[s, :], 4, 0)
    out_ref[...] = wide_ref[...].astype(bf16)


def pair_sum(mine, other):
    return pl.pallas_call(
        pair_kernel,
        in_specs=[VM, VM],
        out_specs=[VM, VM],
        out_shape=[
            jax.ShapeDtypeStruct(mine.shape, f32),
            jax.ShapeDtypeStruct(mine.shape, bf16),
        ],
        compiler_params=params(4),
        name="pair_sum",
    )(mine, other)


def adam_kernel(tall, block, acts_ref, mine_ref, o1, o2, o3, bias_ref, act_ref, s0, s1, s2, s3,
                w_ref, m_ref, v_ref, recon_ref, out_ref, right_ref, scale_ref):
    step = pl.program_id(0)
    total_rows, depth = mine_ref.shape
    local = recon_ref.shape[0]

    @pl.when(step == 0)
    def _():
        others = [o[...].astype(f32) for o in (o1, o2, o3)]
        pieces = []
        for q in range(total_rows // 8):
            piece = mine_ref[8 * q:8 * q + 8, :]
            for k, other in enumerate(others):
                p = q ^ (k + 1)
                piece = piece + other[8 * p:8 * p + 8]
            pieces.append(piece + bias_ref[...])
        rebuilt = jnp.concatenate(pieces, axis=0)
        recon_ref[...] = rebuilt[:local].astype(bf16)
        residual = (rebuilt - acts_ref[...]).astype(bf16)
        scaled = residual.astype(f32) * (A * 2.0 / total_rows)
        high = scaled.astype(bf16)
        low = (scaled - high.astype(f32)).astype(bf16)
        right_ref[...] = jnp.concatenate([high, low], axis=0)
        norm = lax.rsqrt((s0[...] + s1[...]) + (s2[...] + s3[...]) + norm_eps)
        counts = jnp.sum(act_ref[...].astype(f32), axis=0, keepdims=True)
        scale_ref[...] = (A * sparsity_coef / total_rows) * counts * norm

    right = right_ref[...]
    eye = (
        lax.broadcasted_iota(jnp.int32, (block, block), 0)
        == lax.broadcasted_iota(jnp.int32, (block, block), 1)
    )

    @pl.loop(0, tall // block)
    def _(b):
        here = pl.ds(pl.multiple_of(b * block, block), block)
        there = pl.ds(pl.multiple_of(step * tall + b * block, block), block)
        diag = jnp.where(eye, scale_ref[:, there], 0.0).astype(bf16)
        mine = act_ref[:, there].T
        left = jnp.concatenate([diag, mine, mine], axis=1)
        for c in range(0, depth, 256):
            cols = slice(c, min(c + 256, depth))
            both = jnp.concatenate([w_ref[there, cols], right[:, cols]], axis=0)
            g = jnp.dot(left, both, preferred_element_type=f32)
            x = v_ref[here, cols].astype(f32) + g * g
            r = lax.rsqrt(x)
            top = (m_ref[here, cols].astype(f32) + K * g) * r
            out_ref[here, cols] = (top * pltpu.reciprocal(E * r + 1.0 / C, approx=True)).astype(bf16)


def adam(acts, mine, others, bias, act, sums, w, m, v, local, tall=512, block=128):
    width, depth = w.shape
    total = mine.shape[0]
    tile = pl.BlockSpec((tall, depth), lambda i: (i, 0))
    return pl.pallas_call(
        functools.partial(adam_kernel, tall, block),
        grid=(width // tall,),
        in_specs=[VM] * 12 + [tile, tile],
        out_specs=[VM, tile],
        out_shape=[
            jax.ShapeDtypeStruct((local, depth), bf16),
            jax.ShapeDtypeStruct((width, depth), bf16),
        ],
        scratch_shapes=[pltpu.VMEM((2 * total, depth), bf16), pltpu.VMEM((1, width), f32)],
        compiler_params=params(16),
        cost_estimate=cost(8 * total * w.size, 6 * w.size),
        name="adam",
    )(
        acts, mine, *others, bias, act, *sums, w,
        pltpu.with_memory_space_constraint(m, pltpu.HBM),
        pltpu.with_memory_space_constraint(v, pltpu.HBM),
    )


def fast(sizes, activations, enc_weight, enc_bias, dec_weight, dec_bias, first_moment, second_moment):
    feat = sizes[0]
    parts = sizes[1] * sizes[2]
    local = activations.shape[0]
    me = place(PARTS, sizes[1:]).astype(jnp.int32).reshape(1)
    bias = dec_bias.reshape(1, -1)

    mine = activations.astype(f32)
    pair = jnp.concatenate([mine, swap(mine, "feat", feat, 1)], axis=0)
    rows = [pair] + [swap(pair, "feat", feat, k) for k in (2, 4, 6)]
    all_rows, *partials = encode(me, rows, bias, enc_weight, parts)
    partials = [partials[0]] + [swap(partials[k], PARTS, parts, k) for k in range(1, parts)]
    act = activate(me, enc_bias.reshape(1, -1), partials)
    acts = [act] + [swap(act, PARTS, parts, k) for k in range(1, parts)]

    w = pltpu.with_memory_space_constraint(dec_weight, pltpu.VMEM)
    sums = squares(w)
    sums = [sums] + [swap(sums, PARTS, parts, k) for k in range(1, parts)]
    part, all_act = rebuild(me, acts, w)
    part, narrow = pair_sum(part, swap(part, "feat", feat, 1))
    others = [swap(narrow, "feat", feat, k) for k in (2, 4, 6)]
    return adam(all_rows, part, others, bias, all_act, sums, w, first_moment, second_moment, local)


def plain(activations, enc_weight, enc_bias, dec_weight, dec_bias, first_moment, second_moment):
    local_rows = activations.shape[0]
    total_rows = local_rows * lax.axis_size("feat")
    centered = (activations.astype(f32) - dec_bias).astype(bf16)
    partial_value = jnp.dot(
        lax.all_gather(centered, "feat", axis=0, tiled=True), enc_weight, preferred_element_type=f32
    )
    wide = dec_weight.astype(f32)
    squares_sum = jnp.sum(wide * wide, axis=1)
    pre_sum, sum_squares = lax.psum((partial_value, squares_sum), PARTS)
    active = jnp.maximum(pre_sum + enc_bias, 0.0).astype(bf16)
    part = jnp.dot(active, dec_weight, preferred_element_type=f32)
    rebuilt = lax.psum_scatter(part, "feat", scatter_dimension=0, tiled=True) + dec_bias
    residual = (rebuilt - activations.astype(f32)).astype(bf16)
    all_residual = lax.all_gather(residual, "feat", axis=0, tiled=True)
    product = lax.dot_general(
        active, all_residual, (((0,), (0,)), ((), ())), preferred_element_type=f32
    )
    counts = jnp.sum(active.astype(f32), axis=0)
    row_norm = jnp.sqrt(sum_squares + norm_eps)
    gradient = (
        2.0 / total_rows * product
        + sparsity_coef / total_rows * counts[:, None] * wide / row_norm[:, None]
    )
    moment_one = beta_one * first_moment.astype(f32) + (1.0 - beta_one) * gradient
    moment_two = beta_two * second_moment.astype(f32) + (1.0 - beta_two) * gradient * gradient
    dec_step = moment_one / bias_one / (jnp.sqrt(moment_two / bias_two) + adam_eps)
    return rebuilt.astype(bf16), dec_step.astype(bf16)


def solution(mesh):
    sizes = tuple(mesh.shape[name] for name in ("feat", "row", "rep"))

    def shards(*args):
        local, depth = args[0].shape
        width = args[1].shape[1]
        fits = sizes[0] == 8 and local == 4 and depth % 128 == 0
        if fits and width % (1024 * sizes[1] * sizes[2]) == 0 and sizes[1] * sizes[2] == 4:
            return fast(sizes, *args)
        return plain(*args)

    split = P("feat", PARTS)
    return jax.shard_map(
        shards,
        mesh=mesh,
        in_specs=(split, P(PARTS, "feat"), P("feat"), split, P(PARTS), split, split),
        out_specs=(split, split),
        check_vma=False,
    )
```

```python
import functools

import jax
import jax.experimental.pallas as pl
import jax.experimental.pallas.tpu as pltpu
import jax.numpy as jnp
from jax import lax
from jax.sharding import PartitionSpec as P

sparsity_coef = 5.0
beta_one = 0.9
beta_two = 0.999
bias_one = 0.99997344
bias_two = 0.095207853
adam_eps = 1e-08
norm_eps = 1e-06

f32 = jnp.float32
bf16 = jnp.bfloat16
MIB = 1 << 20
TALL = 1024
PARTS = ("row", "rep")
VM = pl.BlockSpec(memory_space=pltpu.VMEM)
HBM = pl.BlockSpec(memory_space=pltpu.HBM)
ANY = pl.BlockSpec(memory_space=pl.ANY)

A = ((1.0 - beta_two) / beta_two) ** 0.5
K = (1.0 - beta_one) / beta_one / A
C = beta_one / bias_one / (beta_two / bias_two) ** 0.5
E = adam_eps * bias_one / beta_one


def params(mib):
    return pltpu.CompilerParams(vmem_limit_bytes=mib * MIB)


def cost(flops, read):
    return pl.CostEstimate(flops=flops, bytes_accessed=read, transcendentals=0)


def swap(x, axis, n, k):
    return lax.ppermute(x, axis, [(a, a ^ k) for a in range(n)])


def place(parts, axis_sizes):
    index = 0
    for name, size in zip(parts, axis_sizes):
        index = index * size + lax.axis_index(name)
    return index


def widen_kernel(x_ref, bias_ref, out_ref, same_ref):
    out_ref[...] = x_ref[...].astype(f32)
    same_ref[...] = bias_ref[...]


def widen(x, bias):
    return pl.pallas_call(
        widen_kernel,
        in_specs=[VM, VM],
        out_specs=[VM, VM],
        out_shape=[jax.ShapeDtypeStruct(x.shape, f32), jax.ShapeDtypeStruct(bias.shape, f32)],
        compiler_params=params(4),
        name="widen",
    )(x, bias)


def join_kernel(mine_ref, other_ref, out_ref):
    out_ref[...] = jnp.concatenate([mine_ref[...], other_ref[...].astype(f32)], axis=0)


def join(mine, other):
    return pl.pallas_call(
        join_kernel,
        in_specs=[VM, VM],
        out_specs=VM,
        out_shape=jax.ShapeDtypeStruct((2 * mine.shape[0], mine.shape[1]), f32),
        compiler_params=params(4),
        name="join",
    )(mine, other)


def center_kernel(*refs):
    rows, (bias_ref, rows_ref, out_ref) = refs[:-3], refs[-3:]
    x = jnp.concatenate([r[...] for r in rows], axis=0)
    rows_ref[...] = x
    out_ref[...] = (x - bias_ref[...]).astype(bf16)


def center(rows, bias):
    shape = (sum(r.shape[0] for r in rows), bias.shape[1])
    return pl.pallas_call(
        center_kernel,
        in_specs=[VM] * (len(rows) + 1),
        out_specs=[VM, VM],
        out_shape=[jax.ShapeDtypeStruct(shape, f32), jax.ShapeDtypeStruct(shape, bf16)],
        compiler_params=params(4),
        name="center",
    )(*rows, bias)


def columns(me_ref, k, chunk):
    return pl.ds(pl.multiple_of(jnp.bitwise_xor(me_ref[0], k) * chunk, 128), chunk)


PIECES = 4


def strip_copies(me_ref, k, w_ref, out_ref, sems, first=0):
    depth, chunk = out_ref.shape
    rows = depth // PIECES
    return [
        pltpu.make_async_copy(
            w_ref.at[pl.ds(p * rows, rows), columns(me_ref, k, chunk)],
            out_ref.at[pl.ds(p * rows, rows)],
            sems.at[first + p],
        )
        for p in range(PIECES)
    ]


def fetch_kernel(ks, me_ref, w_ref, _, *refs):
    outs, sems = refs[:-1], refs[-1]
    copies = []
    for i, (k, out) in enumerate(zip(ks, outs)):
        copies += strip_copies(me_ref, k, w_ref, out, sems, i * PIECES)
    for copy in copies:
        copy.start()
    for copy in copies:
        copy.wait()


def fetch(ks, me, w, after, parts):
    depth, width = w.shape
    return pl.pallas_call(
        functools.partial(fetch_kernel, ks),
        in_specs=[pl.BlockSpec(memory_space=pltpu.SMEM), HBM, ANY],
        out_specs=[VM] * len(ks),
        out_shape=[pltpu.VMEM((depth, width // parts), bf16)] * len(ks),
        scratch_shapes=[pltpu.SemaphoreType.DMA((len(ks) * PIECES,))],
        compiler_params=params(4),
        cost_estimate=cost(0, 2 * len(ks) * depth * width // parts),
        name="fetch",
    )(me, pltpu.with_memory_space_constraint(w, pltpu.HBM), after)


def encode_kernel(ahead, me_ref, x_ref, here_ref, *refs):
    out_ref = refs[-1] if ahead is None else refs[1]
    chunk = out_ref.shape[1]
    wide = 512
    copies = []
    if ahead is not None:
        copies = strip_copies(me_ref, ahead, refs[0], refs[2], refs[3])
    for copy in copies:
        copy.start()

    @pl.loop(0, chunk // wide)
    def _(t):
        s = pl.ds(pl.multiple_of(t * wide, 128), wide)
        out_ref[:, s] = jnp.dot(
            x_ref[...], here_ref[:, s], preferred_element_type=f32
        ).astype(bf16)

    for copy in copies:
        copy.wait()


def encode(me, x, here, w=None, ahead=None):
    total, (depth, chunk) = x.shape[0], here.shape
    out = jax.ShapeDtypeStruct((total, chunk), bf16)
    more = ahead is not None
    return pl.pallas_call(
        functools.partial(encode_kernel, ahead),
        in_specs=[pl.BlockSpec(memory_space=pltpu.SMEM), VM, VM] + [HBM] * more,
        out_specs=[VM, VM] if more else VM,
        out_shape=[out, pltpu.VMEM((depth, chunk), bf16)] if more else out,
        scratch_shapes=[pltpu.SemaphoreType.DMA((PIECES,))] * more,
        compiler_params=params(4),
        cost_estimate=cost(2 * total * depth * chunk, 2 * depth * chunk),
        name="encode",
    )(me, x, here, *([pltpu.with_memory_space_constraint(w, pltpu.HBM)] if more else []))


def active_kernel(me_ref, bias_ref, *refs):
    out = refs[-1]
    chunk = out.shape[1]
    total = refs[0][...].astype(f32)
    for r in refs[1:-1]:
        total = total + r[...].astype(f32)
    start = pl.multiple_of(me_ref[0] * chunk, 128)
    out[...] = jnp.maximum(total + bias_ref[:, pl.ds(start, chunk)], 0.0).astype(bf16)


def activate(me, bias, partials):
    return pl.pallas_call(
        active_kernel,
        in_specs=[pl.BlockSpec(memory_space=pltpu.SMEM)] + [VM] * (len(partials) + 1),
        out_specs=VM,
        out_shape=jax.ShapeDtypeStruct(partials[0].shape, bf16),
        compiler_params=params(4),
        name="activate",
    )(me, bias, *partials)


def squares_kernel(w_ref, _, out_ref):
    tall = 256

    @pl.loop(0, w_ref.shape[0] // TALL)
    def _(i):
        for c in range(0, TALL, tall):
            rows = pl.ds(pl.multiple_of(i * TALL + c, tall), tall)
            total = jnp.zeros((tall, 128), f32)
            for d in range(0, w_ref.shape[1], 128):
                w = w_ref[rows, d:d + 128].astype(f32)
                total = total + w * w
            out_ref[pl.ds(i, 1), c:c + tall] = jnp.sum(total.T, axis=0, keepdims=True)


def squares(w, after):
    return pl.pallas_call(
        squares_kernel,
        in_specs=[VM, ANY],
        out_specs=VM,
        out_shape=jax.ShapeDtypeStruct((w.shape[0] // TALL, TALL), f32),
        compiler_params=params(4),
        cost_estimate=cost(2 * w.size, 2 * w.size),
        name="squares",
    )(w, after)


def rebuild_part(k, me_ref, act_ref, w_ref, total):
    chunk = act_ref.shape[1]
    tall = 1024
    start = jnp.bitwise_xor(me_ref[0], k) * chunk

    def body(t, acc):
        rows = pl.ds(pl.multiple_of(start + t * tall, 128), tall)
        mine = act_ref[:, pl.ds(pl.multiple_of(t * tall, 128), tall)]
        return acc + jnp.dot(mine, w_ref[rows, :], preferred_element_type=f32)

    return lax.fori_loop(0, chunk // tall, body, total)


def rebuild_own_kernel(me_ref, act_ref, w_ref, out_ref):
    out_ref[...] = rebuild_part(0, me_ref, act_ref, w_ref, jnp.zeros(out_ref.shape, f32))


def rebuild_kernel(me_ref, part_ref, *refs):
    acts, w_ref, (out_ref, all_ref, counts_ref) = refs[:-4], refs[-4], refs[-3:]
    chunk = acts[0].shape[1]
    total = part_ref[...]
    for k, act in enumerate(acts):
        here = columns(me_ref, k, chunk)
        all_ref[:, here] = act[...]
        for c in range(0, chunk, TALL):
            row = jnp.bitwise_xor(me_ref[0], k) * (chunk // TALL) + c // TALL
            counts_ref[pl.ds(row, 1), :] = jnp.sum(
                act[:, c:c + TALL].astype(f32), axis=0, keepdims=True
            )
        if k:
            total = rebuild_part(k, me_ref, act, w_ref, total)
    out_ref[...] = total


def rebuild_own(me, act, w):
    (total, chunk), depth = act.shape, w.shape[1]
    return pl.pallas_call(
        rebuild_own_kernel,
        in_specs=[pl.BlockSpec(memory_space=pltpu.SMEM), VM, VM],
        out_specs=VM,
        out_shape=jax.ShapeDtypeStruct((total, depth), f32),
        compiler_params=params(4),
        cost_estimate=cost(2 * total * chunk * depth, 2 * chunk * depth),
        name="rebuild_own",
    )(me, act, w)


def rebuild(me, part, acts, w):
    total, (width, depth) = acts[0].shape[0], w.shape
    return pl.pallas_call(
        rebuild_kernel,
        in_specs=[pl.BlockSpec(memory_space=pltpu.SMEM)] + [VM] * (len(acts) + 2),
        out_specs=[VM] * 3,
        out_shape=[
            jax.ShapeDtypeStruct((total, depth), f32),
            jax.ShapeDtypeStruct((total, width), bf16),
            jax.ShapeDtypeStruct((width // TALL, TALL), f32),
        ],
        compiler_params=params(4),
        cost_estimate=cost(2 * total * w.size, 2 * w.size),
        name="rebuild",
    )(me, part, *acts, w)


def add_kernel(a_ref, b_ref, out_ref):
    out_ref[...] = a_ref[...] + b_ref[...]


def add(a, b):
    return pl.pallas_call(
        add_kernel,
        in_specs=[VM, VM],
        out_specs=VM,
        out_shape=jax.ShapeDtypeStruct(a.shape, a.dtype),
        compiler_params=params(4),
        name="add",
    )(a, b)


def pair_kernel(mine_ref, other_ref, wide_ref, out_ref):
    groups = mine_ref.shape[0] // 8
    for q in range(groups):
        s = slice(8 * q, 8 * q + 8)
        wide_ref[s, :] = mine_ref[s, :] + pltpu.roll(other_ref[s, :], 4, 0)
    out_ref[...] = wide_ref[...].astype(bf16)


def pair_sum(mine, other):
    return pl.pallas_call(
        pair_kernel,
        in_specs=[VM, VM],
        out_specs=[VM, VM],
        out_shape=[
            jax.ShapeDtypeStruct(mine.shape, f32),
            jax.ShapeDtypeStruct(mine.shape, bf16),
        ],
        compiler_params=params(4),
        name="pair_sum",
    )(mine, other)


def adam_kernel(tall, block, acts_ref, mine_ref, o1, o2, o3, bias_ref, act_ref, counts_ref, s0, s1,
                w_ref, m_hbm, v_hbm, recon_ref, out_hbm, right_ref, scale_ref, m_buf, v_buf, out_buf,
                m_sems, v_sems, out_sems):
    total_rows, depth = mine_ref.shape
    local = recon_ref.shape[0]
    steps = w_ref.shape[0] // tall
    slots, out_slots = m_buf.shape[0], out_buf.shape[0]

    def tile(ref, i):
        return ref.at[pl.ds(pl.multiple_of(i * tall, tall), tall)]

    def loads(i):
        slot = lax.rem(i, slots)
        return (
            pltpu.make_async_copy(tile(m_hbm, i), m_buf.at[slot], m_sems.at[slot]),
            pltpu.make_async_copy(tile(v_hbm, i), v_buf.at[slot], v_sems.at[slot]),
        )

    def store(i):
        slot = lax.rem(i, out_slots)
        return pltpu.make_async_copy(out_buf.at[slot], tile(out_hbm, i), out_sems.at[slot])

    for i in range(slots):
        for copy in loads(i):
            copy.start()

    others = [o[...].astype(f32) for o in (o1, o2, o3)]
    pieces = []
    for q in range(total_rows // 8):
        piece = mine_ref[8 * q:8 * q + 8, :]
        for k, other in enumerate(others):
            p = q ^ (k + 1)
            piece = piece + other[8 * p:8 * p + 8]
        pieces.append(piece + bias_ref[...])
    rebuilt = jnp.concatenate(pieces, axis=0)
    recon_ref[...] = rebuilt[:local].astype(bf16)
    residual = (rebuilt - acts_ref[...]).astype(bf16)
    right_ref[...] = (residual.astype(f32) * (A * 2.0 / total_rows)).astype(bf16)
    norm = lax.rsqrt(s0[...] + s1[...] + norm_eps)
    scale = (A * sparsity_coef / total_rows) * counts_ref[...] * norm
    for q in range(scale.shape[0]):
        scale_ref[:, q * TALL:(q + 1) * TALL] = scale[q:q + 1]

    right = right_ref[...]
    eye = (
        lax.broadcasted_iota(jnp.int32, (block, block), 0)
        == lax.broadcasted_iota(jnp.int32, (block, block), 1)
    )

    @pl.loop(0, steps)
    def _(i):
        for copy in loads(i):
            copy.wait()

        @pl.when(i >= out_slots)
        def _():
            store(i - out_slots).wait()

        m_ref, v_ref = m_buf.at[lax.rem(i, slots)], v_buf.at[lax.rem(i, slots)]
        out_ref = out_buf.at[lax.rem(i, out_slots)]
        for b in range(tall // block):
            here = pl.ds(b * block, block)
            there = pl.ds(pl.multiple_of(i * tall + b * block, block), block)
            diag = jnp.where(eye, scale_ref[:, there], 0.0).astype(bf16)
            left = jnp.concatenate([diag, act_ref[:, there].T], axis=1)
            for c in range(0, depth, 256):
                cols = slice(c, min(c + 256, depth))
                both = jnp.concatenate([w_ref[there, cols], right[:, cols]], axis=0)
                g = jnp.dot(left, both, preferred_element_type=f32)
                x = v_ref[here, cols].astype(f32) + g * g
                r = lax.rsqrt(x)
                top = (m_ref[here, cols].astype(f32) + K * g) * r
                step = top * pltpu.reciprocal(E * r + 1.0 / C, approx=True)
                out_ref[here, cols] = step.astype(bf16)
        store(i).start()

        @pl.when(i + slots < steps)
        def _():
            for copy in loads(i + slots):
                copy.start()

    for i in range(steps - out_slots, steps):
        store(i).wait()


def adam(acts, mine, others, bias, act, counts, sums, w, m, v, local, tall=TALL, block=128):
    width, depth = w.shape
    total = mine.shape[0]
    slots, out_slots = 3, 2
    return pl.pallas_call(
        functools.partial(adam_kernel, tall, block),
        in_specs=[VM] * 11 + [HBM, HBM],
        out_specs=[VM, HBM],
        out_shape=[
            jax.ShapeDtypeStruct((local, depth), bf16),
            pltpu.HBM((width, depth), bf16),
        ],
        scratch_shapes=[
            pltpu.VMEM((total, depth), bf16),
            pltpu.VMEM((1, width), f32),
            pltpu.VMEM((slots, tall, depth), bf16),
            pltpu.VMEM((slots, tall, depth), bf16),
            pltpu.VMEM((out_slots, tall, depth), bf16),
            pltpu.SemaphoreType.DMA((slots,)),
            pltpu.SemaphoreType.DMA((slots,)),
            pltpu.SemaphoreType.DMA((out_slots,)),
        ],
        compiler_params=params(21),
        cost_estimate=cost(8 * total * w.size, 6 * w.size),
        name="adam",
    )(
        acts, mine, *others, bias, act, counts, *sums, w,
        pltpu.with_memory_space_constraint(m, pltpu.HBM),
        pltpu.with_memory_space_constraint(v, pltpu.HBM),
    )


def fast(sizes, activations, enc_weight, enc_bias, dec_weight, dec_bias, first_moment, second_moment):
    feat = sizes[0]
    parts = sizes[1] * sizes[2]
    local = activations.shape[0]
    me = place(PARTS, sizes[1:]).astype(jnp.int32).reshape(1)
    near = swap(activations, "feat", feat, 1)
    mine, bias = widen(activations, dec_bias.reshape(1, -1))
    near, mine = lax.optimization_barrier((near, mine))
    pair = join(mine, near)
    rows = [pair] + [swap(pair, "feat", feat, k) for k in (2, 4, 6)]
    w3, w1 = fetch((3, 1), me, enc_weight, pair, parts)
    all_rows, x = center(rows, bias)
    x, w3, w1 = lax.optimization_barrier((x, w3, w1))
    p3, w2 = encode(me, x, w3, enc_weight, ahead=2)
    p1, w0 = encode(me, x, w1, enc_weight, ahead=0)
    p2 = encode(me, x, w2)
    p0 = encode(me, x, w0)
    arrived = [p0] + [swap(p, PARTS, parts, k) for k, p in ((1, p1), (2, p2), (3, p3))]

    w = pltpu.with_memory_space_constraint(dec_weight, pltpu.VMEM)
    sums = squares(w, p0)
    arrived, sums = lax.optimization_barrier((arrived, sums))
    act = activate(me, enc_bias.reshape(1, -1), arrived)
    acts = [act] + [swap(act, PARTS, parts, k) for k in range(1, parts)]
    part = rebuild_own(me, act, w)
    part, sums = lax.optimization_barrier((part, sums))
    sums = add(sums, swap(sums, PARTS, parts, 1))
    part, all_act, counts = rebuild(me, part, acts, w)
    other = swap(part, "feat", feat, 1)
    other, sums = lax.optimization_barrier((other, sums))
    part, narrow = pair_sum(part, other)
    others = [swap(narrow, "feat", feat, k) for k in (2, 4, 6)]
    sums = (sums, swap(sums, PARTS, parts, 2))
    return adam(
        all_rows, part, others, bias, all_act, counts, sums, w, first_moment, second_moment, local
    )


def plain(activations, enc_weight, enc_bias, dec_weight, dec_bias, first_moment, second_moment):
    local_rows = activations.shape[0]
    total_rows = local_rows * lax.axis_size("feat")
    centered = (activations.astype(f32) - dec_bias).astype(bf16)
    partial_value = jnp.dot(
        lax.all_gather(centered, "feat", axis=0, tiled=True), enc_weight, preferred_element_type=f32
    )
    wide = dec_weight.astype(f32)
    squares_sum = jnp.sum(wide * wide, axis=1)
    pre_sum, sum_squares = lax.psum((partial_value, squares_sum), PARTS)
    active = jnp.maximum(pre_sum + enc_bias, 0.0).astype(bf16)
    part = jnp.dot(active, dec_weight, preferred_element_type=f32)
    rebuilt = lax.psum_scatter(part, "feat", scatter_dimension=0, tiled=True) + dec_bias
    residual = (rebuilt - activations.astype(f32)).astype(bf16)
    all_residual = lax.all_gather(residual, "feat", axis=0, tiled=True)
    product = lax.dot_general(
        active, all_residual, (((0,), (0,)), ((), ())), preferred_element_type=f32
    )
    counts = jnp.sum(active.astype(f32), axis=0)
    row_norm = jnp.sqrt(sum_squares + norm_eps)
    gradient = (
        2.0 / total_rows * product
        + sparsity_coef / total_rows * counts[:, None] * wide / row_norm[:, None]
    )
    moment_one = beta_one * first_moment.astype(f32) + (1.0 - beta_one) * gradient
    moment_two = beta_two * second_moment.astype(f32) + (1.0 - beta_two) * gradient * gradient
    dec_step = moment_one / bias_one / (jnp.sqrt(moment_two / bias_two) + adam_eps)
    return rebuilt.astype(bf16), dec_step.astype(bf16)


def solution(mesh):
    sizes = tuple(mesh.shape[name] for name in ("feat", "row", "rep"))

    def shards(*args):
        local, depth = args[0].shape
        width = args[1].shape[1]
        fits = sizes[0] == 8 and local == 4 and depth % 128 == 0
        if fits and width % (TALL * sizes[1] * sizes[2]) == 0 and sizes[1] * sizes[2] == 4:
            return fast(sizes, *args)
        return plain(*args)

    split = P("feat", PARTS)
    return jax.shard_map(
        shards,
        mesh=mesh,
        in_specs=(split, P(PARTS, "feat"), P("feat"), split, P(PARTS), split, split),
        out_specs=(split, split),
        check_vma=False,
    )
```

```python
import functools

import jax
import jax.experimental.pallas as pl
import jax.experimental.pallas.tpu as pltpu
import jax.numpy as jnp
from jax import lax
from jax.sharding import PartitionSpec as P

sparsity_coef = 5.0
beta_one = 0.9
beta_two = 0.999
bias_one = 0.99997344
bias_two = 0.095207853
adam_eps = 1e-08
norm_eps = 1e-06

f32 = jnp.float32
bf16 = jnp.bfloat16
MIB = 1 << 20
TALL = 1024
PARTS = ("row", "rep")
VM = pl.BlockSpec(memory_space=pltpu.VMEM)
HBM = pl.BlockSpec(memory_space=pltpu.HBM)
ANY = pl.BlockSpec(memory_space=pl.ANY)

A = ((1.0 - beta_two) / beta_two) ** 0.5
K = (1.0 - beta_one) / beta_one / A
C = beta_one / bias_one / (beta_two / bias_two) ** 0.5
E = adam_eps * bias_one / beta_one


def params(mib):
    return pltpu.CompilerParams(vmem_limit_bytes=mib * MIB)


def cost(flops, read):
    return pl.CostEstimate(flops=flops, bytes_accessed=read, transcendentals=0)


def swap(x, axis, n, k):
    return lax.ppermute(x, axis, [(a, a ^ k) for a in range(n)])


def place(parts, axis_sizes):
    index = 0
    for name, size in zip(parts, axis_sizes):
        index = index * size + lax.axis_index(name)
    return index


def widen_kernel(x_ref, bias_ref, out_ref, same_ref):
    out_ref[...] = x_ref[...].astype(f32)
    same_ref[...] = bias_ref[...]


def widen(x, bias):
    return pl.pallas_call(
        widen_kernel,
        in_specs=[VM, VM],
        out_specs=[VM, VM],
        out_shape=[jax.ShapeDtypeStruct(x.shape, f32), jax.ShapeDtypeStruct(bias.shape, f32)],
        compiler_params=params(4),
        name="widen",
    )(x, bias)


def join_kernel(mine_ref, other_ref, out_ref):
    out_ref[...] = jnp.concatenate([mine_ref[...], other_ref[...].astype(f32)], axis=0)


def join(mine, other):
    return pl.pallas_call(
        join_kernel,
        in_specs=[VM, VM],
        out_specs=VM,
        out_shape=jax.ShapeDtypeStruct((2 * mine.shape[0], mine.shape[1]), f32),
        compiler_params=params(4),
        name="join",
    )(mine, other)


def center_kernel(*refs):
    rows, (bias_ref, rows_ref, out_ref) = refs[:-3], refs[-3:]
    x = jnp.concatenate([r[...] for r in rows], axis=0)
    rows_ref[...] = x
    out_ref[...] = (x - bias_ref[...]).astype(bf16)


def center(rows, bias):
    shape = (sum(r.shape[0] for r in rows), bias.shape[1])
    return pl.pallas_call(
        center_kernel,
        in_specs=[VM] * (len(rows) + 1),
        out_specs=[VM, VM],
        out_shape=[jax.ShapeDtypeStruct(shape, f32), jax.ShapeDtypeStruct(shape, bf16)],
        compiler_params=params(4),
        name="center",
    )(*rows, bias)


def columns(me_ref, k, chunk):
    return pl.ds(pl.multiple_of(jnp.bitwise_xor(me_ref[0], k) * chunk, 128), chunk)


PIECES = 4


def strip_copies(me_ref, k, w_ref, out_ref, sems, first=0):
    depth, chunk = out_ref.shape
    rows = depth // PIECES
    return [
        pltpu.make_async_copy(
            w_ref.at[pl.ds(p * rows, rows), columns(me_ref, k, chunk)],
            out_ref.at[pl.ds(p * rows, rows)],
            sems.at[first + p],
        )
        for p in range(PIECES)
    ]


def fetch_kernel(ks, me_ref, w_ref, _, *refs):
    outs, sems = refs[:-1], refs[-1]
    copies = []
    for i, (k, out) in enumerate(zip(ks, outs)):
        copies += strip_copies(me_ref, k, w_ref, out, sems, i * PIECES)
    for copy in copies:
        copy.start()
    for copy in copies:
        copy.wait()


def fetch(ks, me, w, after, parts):
    depth, width = w.shape
    return pl.pallas_call(
        functools.partial(fetch_kernel, ks),
        in_specs=[pl.BlockSpec(memory_space=pltpu.SMEM), HBM, ANY],
        out_specs=[VM] * len(ks),
        out_shape=[pltpu.VMEM((depth, width // parts), bf16)] * len(ks),
        scratch_shapes=[pltpu.SemaphoreType.DMA((len(ks) * PIECES,))],
        compiler_params=params(4),
        cost_estimate=cost(0, 2 * len(ks) * depth * width // parts),
        name="fetch",
    )(me, pltpu.with_memory_space_constraint(w, pltpu.HBM), after)


def encode_kernel(ahead, me_ref, x_ref, here_ref, *refs):
    out_ref = refs[-1] if ahead is None else refs[1]
    chunk = out_ref.shape[1]
    wide = 512
    copies = []
    if ahead is not None:
        copies = strip_copies(me_ref, ahead, refs[0], refs[2], refs[3])
    for copy in copies:
        copy.start()

    @pl.loop(0, chunk // wide)
    def _(t):
        s = pl.ds(pl.multiple_of(t * wide, 128), wide)
        out_ref[:, s] = jnp.dot(
            x_ref[...], here_ref[:, s], preferred_element_type=f32
        ).astype(bf16)

    for copy in copies:
        copy.wait()


def encode(me, x, here, w=None, ahead=None):
    total, (depth, chunk) = x.shape[0], here.shape
    out = jax.ShapeDtypeStruct((total, chunk), bf16)
    more = ahead is not None
    return pl.pallas_call(
        functools.partial(encode_kernel, ahead),
        in_specs=[pl.BlockSpec(memory_space=pltpu.SMEM), VM, VM] + [HBM] * more,
        out_specs=[VM, VM] if more else VM,
        out_shape=[out, pltpu.VMEM((depth, chunk), bf16)] if more else out,
        scratch_shapes=[pltpu.SemaphoreType.DMA((PIECES,))] * more,
        compiler_params=params(4),
        cost_estimate=cost(2 * total * depth * chunk, 2 * depth * chunk),
        name="encode",
    )(me, x, here, *([pltpu.with_memory_space_constraint(w, pltpu.HBM)] if more else []))


def active_kernel(me_ref, bias_ref, *refs):
    out = refs[-1]
    chunk = out.shape[1]
    total = refs[0][...].astype(f32)
    for r in refs[1:-1]:
        total = total + r[...].astype(f32)
    start = pl.multiple_of(me_ref[0] * chunk, 128)
    out[...] = jnp.maximum(total + bias_ref[:, pl.ds(start, chunk)], 0.0).astype(bf16)


def activate(me, bias, partials):
    return pl.pallas_call(
        active_kernel,
        in_specs=[pl.BlockSpec(memory_space=pltpu.SMEM)] + [VM] * (len(partials) + 1),
        out_specs=VM,
        out_shape=jax.ShapeDtypeStruct(partials[0].shape, bf16),
        compiler_params=params(4),
        name="activate",
    )(me, bias, *partials)


def squares_kernel(w_ref, _, out_ref):
    tall = 256

    @pl.loop(0, w_ref.shape[0] // TALL)
    def _(i):
        for c in range(0, TALL, tall):
            rows = pl.ds(pl.multiple_of(i * TALL + c, tall), tall)
            total = jnp.zeros((tall, 128), f32)
            for d in range(0, w_ref.shape[1], 128):
                w = w_ref[rows, d:d + 128].astype(f32)
                total = total + w * w
            out_ref[pl.ds(i, 1), c:c + tall] = jnp.sum(total.T, axis=0, keepdims=True)


def squares(w, after):
    return pl.pallas_call(
        squares_kernel,
        in_specs=[VM, ANY],
        out_specs=VM,
        out_shape=jax.ShapeDtypeStruct((w.shape[0] // TALL, TALL), f32),
        compiler_params=params(4),
        cost_estimate=cost(2 * w.size, 2 * w.size),
        name="squares",
    )(w, after)


def rebuild_part(k, me_ref, act_ref, w_ref, total):
    chunk = act_ref.shape[1]
    tall = 1024
    start = jnp.bitwise_xor(me_ref[0], k) * chunk

    def body(t, acc):
        rows = pl.ds(pl.multiple_of(start + t * tall, 128), tall)
        mine = act_ref[:, pl.ds(pl.multiple_of(t * tall, 128), tall)]
        return acc + jnp.dot(mine, w_ref[rows, :], preferred_element_type=f32)

    return lax.fori_loop(0, chunk // tall, body, total)


def rebuild_own_kernel(me_ref, act_ref, w_ref, out_ref):
    out_ref[...] = rebuild_part(0, me_ref, act_ref, w_ref, jnp.zeros(out_ref.shape, f32))


def rebuild_kernel(me_ref, part_ref, *refs):
    acts, w_ref, (out_ref, all_ref, counts_ref) = refs[:-4], refs[-4], refs[-3:]
    chunk = acts[0].shape[1]
    total = part_ref[...]
    for k, act in enumerate(acts):
        here = columns(me_ref, k, chunk)
        all_ref[:, here] = act[...]
        for c in range(0, chunk, TALL):
            row = jnp.bitwise_xor(me_ref[0], k) * (chunk // TALL) + c // TALL
            counts_ref[pl.ds(row, 1), :] = jnp.sum(
                act[:, c:c + TALL].astype(f32), axis=0, keepdims=True
            )
        if k:
            total = rebuild_part(k, me_ref, act, w_ref, total)
    out_ref[...] = total


def rebuild_own(me, act, w):
    (total, chunk), depth = act.shape, w.shape[1]
    return pl.pallas_call(
        rebuild_own_kernel,
        in_specs=[pl.BlockSpec(memory_space=pltpu.SMEM), VM, VM],
        out_specs=VM,
        out_shape=jax.ShapeDtypeStruct((total, depth), f32),
        compiler_params=params(4),
        cost_estimate=cost(2 * total * chunk * depth, 2 * chunk * depth),
        name="rebuild_own",
    )(me, act, w)


def rebuild(me, part, acts, w):
    total, (width, depth) = acts[0].shape[0], w.shape
    return pl.pallas_call(
        rebuild_kernel,
        in_specs=[pl.BlockSpec(memory_space=pltpu.SMEM)] + [VM] * (len(acts) + 2),
        out_specs=[VM] * 3,
        out_shape=[
            jax.ShapeDtypeStruct((total, depth), f32),
            jax.ShapeDtypeStruct((total, width), bf16),
            jax.ShapeDtypeStruct((width // TALL, TALL), f32),
        ],
        compiler_params=params(4),
        cost_estimate=cost(2 * total * w.size, 2 * w.size),
        name="rebuild",
    )(me, part, *acts, w)


def add_kernel(a_ref, b_ref, out_ref):
    out_ref[...] = a_ref[...] + b_ref[...]


def add(a, b):
    return pl.pallas_call(
        add_kernel,
        in_specs=[VM, VM],
        out_specs=VM,
        out_shape=jax.ShapeDtypeStruct(a.shape, a.dtype),
        compiler_params=params(4),
        name="add",
    )(a, b)


def pair_kernel(mine_ref, other_ref, wide_ref, out_ref):
    groups = mine_ref.shape[0] // 8
    for q in range(groups):
        s = slice(8 * q, 8 * q + 8)
        wide_ref[s, :] = mine_ref[s, :] + pltpu.roll(other_ref[s, :], 4, 0)
    out_ref[...] = wide_ref[...].astype(bf16)


def pair_sum(mine, other):
    return pl.pallas_call(
        pair_kernel,
        in_specs=[VM, VM],
        out_specs=[VM, VM],
        out_shape=[
            jax.ShapeDtypeStruct(mine.shape, f32),
            jax.ShapeDtypeStruct(mine.shape, bf16),
        ],
        compiler_params=params(4),
        name="pair_sum",
    )(mine, other)


def adam_kernel(tall, block, acts_ref, mine_ref, o1, o2, o3, bias_ref, act_ref, counts_ref, s0, s1,
                w_ref, m0_ref, v0_ref, m_hbm, v_hbm, recon_ref, out_hbm, right_ref, scale_ref, m_buf, v_buf, out_buf,
                m_sems, v_sems, out_sems):
    total_rows, depth = mine_ref.shape
    local = recon_ref.shape[0]
    steps = w_ref.shape[0] // tall
    slots, out_slots = m_buf.shape[0], out_buf.shape[0]

    def tile(ref, i):
        return ref.at[pl.ds(pl.multiple_of(i * tall, tall), tall)]

    def loads(i):
        slot = lax.rem(i, slots)
        return (
            pltpu.make_async_copy(tile(m_hbm, i), m_buf.at[slot], m_sems.at[slot]),
            pltpu.make_async_copy(tile(v_hbm, i), v_buf.at[slot], v_sems.at[slot]),
        )

    def store(i):
        slot = lax.rem(i, out_slots)
        return pltpu.make_async_copy(out_buf.at[slot], tile(out_hbm, i), out_sems.at[slot])

    early = m0_ref.shape[0] // tall
    for i in range(early, early + slots):
        for copy in loads(i):
            copy.start()

    others = [o[...].astype(f32) for o in (o1, o2, o3)]
    pieces = []
    for q in range(total_rows // 8):
        piece = mine_ref[8 * q:8 * q + 8, :]
        for k, other in enumerate(others):
            p = q ^ (k + 1)
            piece = piece + other[8 * p:8 * p + 8]
        pieces.append(piece + bias_ref[...])
    rebuilt = jnp.concatenate(pieces, axis=0)
    recon_ref[...] = rebuilt[:local].astype(bf16)
    residual = (rebuilt - acts_ref[...]).astype(bf16)
    right_ref[...] = (residual.astype(f32) * (A * 2.0 / total_rows)).astype(bf16)
    norm = lax.rsqrt(s0[...] + s1[...] + norm_eps)
    scale = (A * sparsity_coef / total_rows) * counts_ref[...] * norm
    for q in range(scale.shape[0]):
        scale_ref[:, q * TALL:(q + 1) * TALL] = scale[q:q + 1]

    right = right_ref[...]
    eye = (
        lax.broadcasted_iota(jnp.int32, (block, block), 0)
        == lax.broadcasted_iota(jnp.int32, (block, block), 1)
    )

    def compute(i, m_ref, v_ref):
        out_ref = out_buf.at[lax.rem(i, out_slots)]
        for b in range(tall // block):
            here = pl.ds(b * block, block)
            there = pl.ds(pl.multiple_of(i * tall + b * block, block), block)
            diag = jnp.where(eye, scale_ref[:, there], 0.0).astype(bf16)
            left = jnp.concatenate([diag, act_ref[:, there].T], axis=1)
            for c in range(0, depth, 256):
                cols = slice(c, min(c + 256, depth))
                both = jnp.concatenate([w_ref[there, cols], right[:, cols]], axis=0)
                g = jnp.dot(left, both, preferred_element_type=f32)
                x = v_ref[here, cols].astype(f32) + g * g
                r = lax.rsqrt(x)
                top = (m_ref[here, cols].astype(f32) + K * g) * r
                step = top * pltpu.reciprocal(E * r + 1.0 / C, approx=True)
                out_ref[here, cols] = step.astype(bf16)
        store(i).start()

    @pl.loop(0, early)
    def _(i):
        compute(i, tile(m0_ref, i), tile(v0_ref, i))

    @pl.loop(early, steps)
    def _(i):
        for copy in loads(i):
            copy.wait()

        @pl.when(i >= out_slots)
        def _():
            store(i - out_slots).wait()

        slot = lax.rem(i, slots)
        compute(i, m_buf.at[slot], v_buf.at[slot])

        @pl.when(i + slots < steps)
        def _():
            for copy in loads(i + slots):
                copy.start()

    for i in range(steps - out_slots, steps):
        store(i).wait()


def fill_kernel(m_hbm, v_hbm, _, m_ref, v_ref, sems):
    rows = m_ref.shape[0] // PIECES
    copies = []
    for p in range(PIECES):
        s = pl.ds(p * rows, rows)
        copies.append(pltpu.make_async_copy(m_hbm.at[s], m_ref.at[s], sems.at[0, p]))
        copies.append(pltpu.make_async_copy(v_hbm.at[s], v_ref.at[s], sems.at[1, p]))
    for copy in copies:
        copy.start()
    for copy in copies:
        copy.wait()


def fill(rows, m, v, after):
    out = pltpu.VMEM((rows, m.shape[1]), bf16)
    return pl.pallas_call(
        fill_kernel,
        in_specs=[HBM, HBM, ANY],
        out_specs=[VM, VM],
        out_shape=[out, out],
        scratch_shapes=[pltpu.SemaphoreType.DMA((2, PIECES))],
        compiler_params=params(4),
        cost_estimate=cost(0, 4 * rows * m.shape[1]),
        name="fill",
    )(
        pltpu.with_memory_space_constraint(m, pltpu.HBM),
        pltpu.with_memory_space_constraint(v, pltpu.HBM),
        after,
    )


def adam(acts, mine, others, bias, act, counts, sums, w, first, m, v, local, tall=TALL, block=128):
    width, depth = w.shape
    total = mine.shape[0]
    slots, out_slots = 3, 2
    return pl.pallas_call(
        functools.partial(adam_kernel, tall, block),
        in_specs=[VM] * 13 + [HBM, HBM],
        out_specs=[VM, HBM],
        out_shape=[
            jax.ShapeDtypeStruct((local, depth), bf16),
            pltpu.HBM((width, depth), bf16),
        ],
        scratch_shapes=[
            pltpu.VMEM((total, depth), bf16),
            pltpu.VMEM((1, width), f32),
            pltpu.VMEM((slots, tall, depth), bf16),
            pltpu.VMEM((slots, tall, depth), bf16),
            pltpu.VMEM((out_slots, tall, depth), bf16),
            pltpu.SemaphoreType.DMA((slots,)),
            pltpu.SemaphoreType.DMA((slots,)),
            pltpu.SemaphoreType.DMA((out_slots,)),
        ],
        compiler_params=params(21),
        cost_estimate=cost(8 * total * w.size, 6 * w.size),
        name="adam",
    )(
        acts, mine, *others, bias, act, counts, *sums, w, *first,
        pltpu.with_memory_space_constraint(m, pltpu.HBM),
        pltpu.with_memory_space_constraint(v, pltpu.HBM),
    )


def fast(sizes, activations, enc_weight, enc_bias, dec_weight, dec_bias, first_moment, second_moment):
    feat = sizes[0]
    parts = sizes[1] * sizes[2]
    local = activations.shape[0]
    me = place(PARTS, sizes[1:]).astype(jnp.int32).reshape(1)
    near = swap(activations, "feat", feat, 1)
    mine, bias = widen(activations, dec_bias.reshape(1, -1))
    near, mine = lax.optimization_barrier((near, mine))
    pair = join(mine, near)
    rows = [pair] + [swap(pair, "feat", feat, k) for k in (2, 4, 6)]
    w3, w1 = fetch((3, 1), me, enc_weight, pair, parts)
    all_rows, x = center(rows, bias)
    x, w3, w1 = lax.optimization_barrier((x, w3, w1))
    p3, w2 = encode(me, x, w3, enc_weight, ahead=2)
    p1, w0 = encode(me, x, w1, enc_weight, ahead=0)
    p2 = encode(me, x, w2)
    arrived = [swap(p, PARTS, parts, k) for k, p in ((1, p1), (2, p2), (3, p3))]
    x, arrived[2] = lax.optimization_barrier((x, arrived[2]))
    p0 = encode(me, x, w0)
    arrived = [p0] + arrived

    w = pltpu.with_memory_space_constraint(dec_weight, pltpu.VMEM)
    sums = squares(w, p0)
    arrived, sums = lax.optimization_barrier((arrived, sums))
    act = activate(me, enc_bias.reshape(1, -1), arrived)
    act, sums = lax.optimization_barrier((act, sums))
    acts = [act] + [swap(act, PARTS, parts, k) for k in range(1, parts)]
    sums = add(sums, swap(sums, PARTS, parts, 1))
    part = rebuild_own(me, act, w)
    acts, sums = lax.optimization_barrier((acts, sums))
    part, all_act, counts = rebuild(me, part, acts, w)
    part, narrow = pair_sum(part, swap(part, "feat", feat, 1))
    others = [swap(narrow, "feat", feat, k) for k in (2, 4, 6)]
    sums = (sums, swap(sums, PARTS, parts, 2))
    first = fill(2 * TALL, first_moment, second_moment, narrow)
    return adam(
        all_rows, part, others, bias, all_act, counts, sums, w, first, first_moment,
        second_moment, local,
    )


def plain(activations, enc_weight, enc_bias, dec_weight, dec_bias, first_moment, second_moment):
    local_rows = activations.shape[0]
    total_rows = local_rows * lax.axis_size("feat")
    centered = (activations.astype(f32) - dec_bias).astype(bf16)
    partial_value = jnp.dot(
        lax.all_gather(centered, "feat", axis=0, tiled=True), enc_weight, preferred_element_type=f32
    )
    wide = dec_weight.astype(f32)
    squares_sum = jnp.sum(wide * wide, axis=1)
    pre_sum, sum_squares = lax.psum((partial_value, squares_sum), PARTS)
    active = jnp.maximum(pre_sum + enc_bias, 0.0).astype(bf16)
    part = jnp.dot(active, dec_weight, preferred_element_type=f32)
    rebuilt = lax.psum_scatter(part, "feat", scatter_dimension=0, tiled=True) + dec_bias
    residual = (rebuilt - activations.astype(f32)).astype(bf16)
    all_residual = lax.all_gather(residual, "feat", axis=0, tiled=True)
    product = lax.dot_general(
        active, all_residual, (((0,), (0,)), ((), ())), preferred_element_type=f32
    )
    counts = jnp.sum(active.astype(f32), axis=0)
    row_norm = jnp.sqrt(sum_squares + norm_eps)
    gradient = (
        2.0 / total_rows * product
        + sparsity_coef / total_rows * counts[:, None] * wide / row_norm[:, None]
    )
    moment_one = beta_one * first_moment.astype(f32) + (1.0 - beta_one) * gradient
    moment_two = beta_two * second_moment.astype(f32) + (1.0 - beta_two) * gradient * gradient
    dec_step = moment_one / bias_one / (jnp.sqrt(moment_two / bias_two) + adam_eps)
    return rebuilt.astype(bf16), dec_step.astype(bf16)


def solution(mesh):
    sizes = tuple(mesh.shape[name] for name in ("feat", "row", "rep"))

    def shards(*args):
        local, depth = args[0].shape
        width = args[1].shape[1]
        fits = sizes[0] == 8 and local == 4 and depth % 128 == 0
        if fits and width % (TALL * sizes[1] * sizes[2]) == 0 and sizes[1] * sizes[2] == 4:
            return fast(sizes, *args)
        return plain(*args)

    split = P("feat", PARTS)
    return jax.shard_map(
        shards,
        mesh=mesh,
        in_specs=(split, P(PARTS, "feat"), P("feat"), split, P(PARTS), split, split),
        out_specs=(split, split),
        check_vma=False,
    )
```

```python
import functools

import jax
import jax.experimental.pallas as pl
import jax.experimental.pallas.tpu as pltpu
import jax.numpy as jnp
from jax import lax
from jax.sharding import PartitionSpec as P

sparsity_coef = 5.0
beta_one = 0.9
beta_two = 0.999
bias_one = 0.99997344
bias_two = 0.095207853
adam_eps = 1e-08
norm_eps = 1e-06

f32 = jnp.float32
bf16 = jnp.bfloat16
MIB = 1 << 20
TALL = 1024
EARLY = 2
PARTS = ("row", "rep")
VM = pl.BlockSpec(memory_space=pltpu.VMEM)
HBM = pl.BlockSpec(memory_space=pltpu.HBM)
ANY = pl.BlockSpec(memory_space=pl.ANY)

A = ((1.0 - beta_two) / beta_two) ** 0.5
K = (1.0 - beta_one) / beta_one / A
C = beta_one / bias_one / (beta_two / bias_two) ** 0.5
E = adam_eps * bias_one / beta_one


def params(mib):
    return pltpu.CompilerParams(vmem_limit_bytes=mib * MIB)


def cost(flops, read):
    return pl.CostEstimate(flops=flops, bytes_accessed=read, transcendentals=0)


def swap(x, axis, n, k):
    return lax.ppermute(x, axis, [(a, a ^ k) for a in range(n)])


def place(parts, axis_sizes):
    index = 0
    for name, size in zip(parts, axis_sizes):
        index = index * size + lax.axis_index(name)
    return index


def widen_kernel(x_ref, bias_ref, out_ref, same_ref):
    out_ref[...] = x_ref[...].astype(f32)
    same_ref[...] = bias_ref[...]


def widen(x, bias):
    return pl.pallas_call(
        widen_kernel,
        in_specs=[VM, VM],
        out_specs=[VM, VM],
        out_shape=[jax.ShapeDtypeStruct(x.shape, f32), jax.ShapeDtypeStruct(bias.shape, f32)],
        compiler_params=params(4),
        name="widen",
    )(x, bias)


def join_kernel(mine_ref, other_ref, out_ref):
    out_ref[...] = jnp.concatenate([mine_ref[...], other_ref[...].astype(f32)], axis=0)


def join(mine, other):
    return pl.pallas_call(
        join_kernel,
        in_specs=[VM, VM],
        out_specs=VM,
        out_shape=jax.ShapeDtypeStruct((2 * mine.shape[0], mine.shape[1]), f32),
        compiler_params=params(4),
        name="join",
    )(mine, other)


def center_kernel(*refs):
    rows, (bias_ref, rows_ref, out_ref) = refs[:-3], refs[-3:]
    x = jnp.concatenate([r[...] for r in rows], axis=0)
    rows_ref[...] = x
    out_ref[...] = (x - bias_ref[...]).astype(bf16)


def center(rows, bias):
    shape = (sum(r.shape[0] for r in rows), bias.shape[1])
    return pl.pallas_call(
        center_kernel,
        in_specs=[VM] * (len(rows) + 1),
        out_specs=[VM, VM],
        out_shape=[jax.ShapeDtypeStruct(shape, f32), jax.ShapeDtypeStruct(shape, bf16)],
        compiler_params=params(4),
        name="center",
    )(*rows, bias)


def columns(me_ref, k, chunk):
    return pl.ds(pl.multiple_of(jnp.bitwise_xor(me_ref[0], k) * chunk, 128), chunk)


PIECES = 4


def strip_copies(me_ref, k, w_ref, out_ref, sems, first=0):
    depth, chunk = out_ref.shape
    rows = depth // PIECES
    return [
        pltpu.make_async_copy(
            w_ref.at[pl.ds(p * rows, rows), columns(me_ref, k, chunk)],
            out_ref.at[pl.ds(p * rows, rows)],
            sems.at[first + p],
        )
        for p in range(PIECES)
    ]


def fetch_kernel(ks, me_ref, w_ref, _, *refs):
    outs, sems = refs[:-1], refs[-1]
    copies = []
    for i, (k, out) in enumerate(zip(ks, outs)):
        copies += strip_copies(me_ref, k, w_ref, out, sems, i * PIECES)
    for copy in copies:
        copy.start()
    for copy in copies:
        copy.wait()


def fetch(ks, me, w, after, parts):
    depth, width = w.shape
    return pl.pallas_call(
        functools.partial(fetch_kernel, ks),
        in_specs=[pl.BlockSpec(memory_space=pltpu.SMEM), HBM, ANY],
        out_specs=[VM] * len(ks),
        out_shape=[pltpu.VMEM((depth, width // parts), bf16)] * len(ks),
        scratch_shapes=[pltpu.SemaphoreType.DMA((len(ks) * PIECES,))],
        compiler_params=params(4),
        cost_estimate=cost(0, 2 * len(ks) * depth * width // parts),
        name="fetch",
    )(me, pltpu.with_memory_space_constraint(w, pltpu.HBM), after)


def encode_kernel(ahead, me_ref, x_ref, here_ref, *refs):
    out_ref = refs[-1] if ahead is None else refs[1]
    chunk = out_ref.shape[1]
    wide = 512
    copies = []
    if ahead is not None:
        copies = strip_copies(me_ref, ahead, refs[0], refs[2], refs[3])
    for copy in copies:
        copy.start()

    @pl.loop(0, chunk // wide)
    def _(t):
        s = pl.ds(pl.multiple_of(t * wide, 128), wide)
        out_ref[:, s] = jnp.dot(
            x_ref[...], here_ref[:, s], preferred_element_type=f32
        ).astype(bf16)

    for copy in copies:
        copy.wait()


def encode(me, x, here, w=None, ahead=None):
    total, (depth, chunk) = x.shape[0], here.shape
    out = jax.ShapeDtypeStruct((total, chunk), bf16)
    more = ahead is not None
    return pl.pallas_call(
        functools.partial(encode_kernel, ahead),
        in_specs=[pl.BlockSpec(memory_space=pltpu.SMEM), VM, VM] + [HBM] * more,
        out_specs=[VM, VM] if more else VM,
        out_shape=[out, pltpu.VMEM((depth, chunk), bf16)] if more else out,
        scratch_shapes=[pltpu.SemaphoreType.DMA((PIECES,))] * more,
        compiler_params=params(4),
        cost_estimate=cost(2 * total * depth * chunk, 2 * depth * chunk),
        name="encode",
    )(me, x, here, *([pltpu.with_memory_space_constraint(w, pltpu.HBM)] if more else []))


def active_kernel(me_ref, bias_ref, *refs):
    out = refs[-1]
    chunk = out.shape[1]
    total = refs[0][...].astype(f32)
    for r in refs[1:-1]:
        total = total + r[...].astype(f32)
    start = pl.multiple_of(me_ref[0] * chunk, 128)
    out[...] = jnp.maximum(total + bias_ref[:, pl.ds(start, chunk)], 0.0).astype(bf16)


def activate(me, bias, partials):
    return pl.pallas_call(
        active_kernel,
        in_specs=[pl.BlockSpec(memory_space=pltpu.SMEM)] + [VM] * (len(partials) + 1),
        out_specs=VM,
        out_shape=jax.ShapeDtypeStruct(partials[0].shape, bf16),
        compiler_params=params(4),
        name="activate",
    )(me, bias, *partials)


def squares_kernel(w_ref, _, out_ref):
    tall = 256

    @pl.loop(0, w_ref.shape[0] // TALL)
    def _(i):
        for c in range(0, TALL, tall):
            rows = pl.ds(pl.multiple_of(i * TALL + c, tall), tall)
            total = jnp.zeros((tall, 128), f32)
            for d in range(0, w_ref.shape[1], 128):
                w = w_ref[rows, d:d + 128].astype(f32)
                total = total + w * w
            out_ref[pl.ds(i, 1), c:c + tall] = jnp.sum(total.T, axis=0, keepdims=True)


def squares(w, after):
    return pl.pallas_call(
        squares_kernel,
        in_specs=[VM, ANY],
        out_specs=VM,
        out_shape=jax.ShapeDtypeStruct((w.shape[0] // TALL, TALL), f32),
        compiler_params=params(4),
        cost_estimate=cost(2 * w.size, 2 * w.size),
        name="squares",
    )(w, after)


def rebuild_part(k, me_ref, act_ref, w_ref, total):
    chunk = act_ref.shape[1]
    tall = 1024
    start = jnp.bitwise_xor(me_ref[0], k) * chunk

    def body(t, acc):
        rows = pl.ds(pl.multiple_of(start + t * tall, 128), tall)
        mine = act_ref[:, pl.ds(pl.multiple_of(t * tall, 128), tall)]
        return acc + jnp.dot(mine, w_ref[rows, :], preferred_element_type=f32)

    return lax.fori_loop(0, chunk // tall, body, total)


def rebuild_one_kernel(k, me_ref, act_ref, w_ref, *refs):
    out_ref = refs[-1]
    total = refs[0][...] if len(refs) > 1 else jnp.zeros(out_ref.shape, f32)
    out_ref[...] = rebuild_part(k, me_ref, act_ref, w_ref, total)


def rebuild_kernel(ks, me_ref, part_ref, *refs):
    acts, w_ref, (out_ref, all_ref, counts_ref) = refs[:-4], refs[-4], refs[-3:]
    chunk = acts[0].shape[1]
    total = part_ref[...]
    for k, act in enumerate(acts):
        here = columns(me_ref, k, chunk)
        all_ref[:, here] = act[...]
        for c in range(0, chunk, TALL):
            row = jnp.bitwise_xor(me_ref[0], k) * (chunk // TALL) + c // TALL
            counts_ref[pl.ds(row, 1), :] = jnp.sum(
                act[:, c:c + TALL].astype(f32), axis=0, keepdims=True
            )
        if k in ks:
            total = rebuild_part(k, me_ref, act, w_ref, total)
    out_ref[...] = total


def rebuild_one(k, me, act, w, *part):
    (total, chunk), depth = act.shape, w.shape[1]
    return pl.pallas_call(
        functools.partial(rebuild_one_kernel, k),
        in_specs=[pl.BlockSpec(memory_space=pltpu.SMEM), VM, VM] + [VM] * len(part),
        out_specs=VM,
        out_shape=jax.ShapeDtypeStruct((total, depth), f32),
        compiler_params=params(4),
        cost_estimate=cost(2 * total * chunk * depth, 2 * chunk * depth),
        name="rebuild_one",
    )(me, act, w, *part)


def rebuild(ks, me, part, acts, w):
    total, (width, depth) = acts[0].shape[0], w.shape
    return pl.pallas_call(
        functools.partial(rebuild_kernel, ks),
        in_specs=[pl.BlockSpec(memory_space=pltpu.SMEM)] + [VM] * (len(acts) + 2),
        out_specs=[VM] * 3,
        out_shape=[
            jax.ShapeDtypeStruct((total, depth), f32),
            jax.ShapeDtypeStruct((total, width), bf16),
            jax.ShapeDtypeStruct((width // TALL, TALL), f32),
        ],
        compiler_params=params(4),
        cost_estimate=cost(2 * total * w.size, 2 * w.size),
        name="rebuild",
    )(me, part, *acts, w)


def add_kernel(a_ref, b_ref, out_ref):
    out_ref[...] = a_ref[...] + b_ref[...]


def add(a, b):
    return pl.pallas_call(
        add_kernel,
        in_specs=[VM, VM],
        out_specs=VM,
        out_shape=jax.ShapeDtypeStruct(a.shape, a.dtype),
        compiler_params=params(4),
        name="add",
    )(a, b)


def pair_kernel(mine_ref, other_ref, wide_ref, out_ref):
    groups = mine_ref.shape[0] // 8
    for q in range(groups):
        s = slice(8 * q, 8 * q + 8)
        wide_ref[s, :] = mine_ref[s, :] + pltpu.roll(other_ref[s, :], 4, 0)
    out_ref[...] = wide_ref[...].astype(bf16)


def pair_sum(mine, other):
    return pl.pallas_call(
        pair_kernel,
        in_specs=[VM, VM],
        out_specs=[VM, VM],
        out_shape=[
            jax.ShapeDtypeStruct(mine.shape, f32),
            jax.ShapeDtypeStruct(mine.shape, bf16),
        ],
        compiler_params=params(4),
        name="pair_sum",
    )(mine, other)


def adam_kernel(tall, block, acts_ref, mine_ref, o1, o2, o3, bias_ref, act_ref, counts_ref, s0, s1,
                w_ref, m0_ref, v0_ref, m_hbm, v_hbm, recon_ref, out_hbm, right_ref, scale_ref, m_buf, v_buf, out_buf,
                m_sems, v_sems, out_sems):
    total_rows, depth = mine_ref.shape
    local = recon_ref.shape[0]
    steps = w_ref.shape[0] // tall
    slots, out_slots = m_buf.shape[0], out_buf.shape[0]

    def tile(ref, i):
        return ref.at[pl.ds(pl.multiple_of(i * tall, tall), tall)]

    def loads(i):
        slot = lax.rem(i, slots)
        return (
            pltpu.make_async_copy(tile(m_hbm, i), m_buf.at[slot], m_sems.at[slot]),
            pltpu.make_async_copy(tile(v_hbm, i), v_buf.at[slot], v_sems.at[slot]),
        )

    def store(i):
        slot = lax.rem(i, out_slots)
        return pltpu.make_async_copy(out_buf.at[slot], tile(out_hbm, i), out_sems.at[slot])

    early = m0_ref.shape[0] // tall
    for i in range(early, early + slots):
        for copy in loads(i):
            copy.start()

    others = [o[...].astype(f32) for o in (o1, o2, o3)]
    pieces = []
    for q in range(total_rows // 8):
        piece = mine_ref[8 * q:8 * q + 8, :]
        for k, other in enumerate(others):
            p = q ^ (k + 1)
            piece = piece + other[8 * p:8 * p + 8]
        pieces.append(piece + bias_ref[...])
    rebuilt = jnp.concatenate(pieces, axis=0)
    recon_ref[...] = rebuilt[:local].astype(bf16)
    residual = (rebuilt - acts_ref[...]).astype(bf16)
    right_ref[...] = (residual.astype(f32) * (A * 2.0 / total_rows)).astype(bf16)
    norm = lax.rsqrt(s0[...] + s1[...] + norm_eps)
    scale = (A * sparsity_coef / total_rows) * counts_ref[...] * norm
    for q in range(scale.shape[0]):
        scale_ref[:, q * TALL:(q + 1) * TALL] = scale[q:q + 1]

    right = right_ref[...]
    eye = (
        lax.broadcasted_iota(jnp.int32, (block, block), 0)
        == lax.broadcasted_iota(jnp.int32, (block, block), 1)
    )

    def compute(i, m_ref, v_ref):
        out_ref = out_buf.at[lax.rem(i, out_slots)]
        for b in range(tall // block):
            here = pl.ds(b * block, block)
            there = pl.ds(pl.multiple_of(i * tall + b * block, block), block)
            diag = jnp.where(eye, scale_ref[:, there], 0.0).astype(bf16)
            left = jnp.concatenate([diag, act_ref[:, there].T], axis=1)
            for c in range(0, depth, 256):
                cols = slice(c, min(c + 256, depth))
                both = jnp.concatenate([w_ref[there, cols], right[:, cols]], axis=0)
                g = jnp.dot(left, both, preferred_element_type=f32)
                x = v_ref[here, cols].astype(f32) + g * g
                r = lax.rsqrt(x)
                top = (m_ref[here, cols].astype(f32) + K * g) * r
                step = top * pltpu.reciprocal(E * r + 1.0 / C, approx=True)
                out_ref[here, cols] = step.astype(bf16)
        store(i).start()

    @pl.loop(0, early)
    def _(i):
        compute(i, tile(m0_ref, i), tile(v0_ref, i))

    @pl.loop(early, steps)
    def _(i):
        for copy in loads(i):
            copy.wait()

        @pl.when(i >= out_slots)
        def _():
            store(i - out_slots).wait()

        slot = lax.rem(i, slots)
        compute(i, m_buf.at[slot], v_buf.at[slot])

        @pl.when(i + slots < steps)
        def _():
            for copy in loads(i + slots):
                copy.start()

    for i in range(steps - out_slots, steps):
        store(i).wait()


def fill_kernel(m_hbm, v_hbm, _, m_ref, v_ref, sems):
    rows = m_ref.shape[0] // PIECES
    copies = []
    for p in range(PIECES):
        s = pl.ds(p * rows, rows)
        copies.append(pltpu.make_async_copy(m_hbm.at[s], m_ref.at[s], sems.at[0, p]))
        copies.append(pltpu.make_async_copy(v_hbm.at[s], v_ref.at[s], sems.at[1, p]))
    for copy in copies:
        copy.start()
    for copy in copies:
        copy.wait()


def fill(rows, m, v, after):
    out = pltpu.VMEM((rows, m.shape[1]), bf16)
    return pl.pallas_call(
        fill_kernel,
        in_specs=[HBM, HBM, ANY],
        out_specs=[VM, VM],
        out_shape=[out, out],
        scratch_shapes=[pltpu.SemaphoreType.DMA((2, PIECES))],
        compiler_params=params(4),
        cost_estimate=cost(0, 4 * rows * m.shape[1]),
        name="fill",
    )(
        pltpu.with_memory_space_constraint(m, pltpu.HBM),
        pltpu.with_memory_space_constraint(v, pltpu.HBM),
        after,
    )


def adam(acts, mine, others, bias, act, counts, sums, w, first, m, v, local, tall=TALL, block=128):
    width, depth = w.shape
    total = mine.shape[0]
    slots, out_slots = 3, 2
    return pl.pallas_call(
        functools.partial(adam_kernel, tall, block),
        in_specs=[VM] * 13 + [HBM, HBM],
        out_specs=[VM, HBM],
        out_shape=[
            jax.ShapeDtypeStruct((local, depth), bf16),
            pltpu.HBM((width, depth), bf16),
        ],
        scratch_shapes=[
            pltpu.VMEM((total, depth), bf16),
            pltpu.VMEM((1, width), f32),
            pltpu.VMEM((slots, tall, depth), bf16),
            pltpu.VMEM((slots, tall, depth), bf16),
            pltpu.VMEM((out_slots, tall, depth), bf16),
            pltpu.SemaphoreType.DMA((slots,)),
            pltpu.SemaphoreType.DMA((slots,)),
            pltpu.SemaphoreType.DMA((out_slots,)),
        ],
        compiler_params=params(21),
        cost_estimate=cost(8 * total * w.size, 6 * w.size),
        name="adam",
    )(
        acts, mine, *others, bias, act, counts, *sums, w, *first,
        pltpu.with_memory_space_constraint(m, pltpu.HBM),
        pltpu.with_memory_space_constraint(v, pltpu.HBM),
    )


def fast(sizes, activations, enc_weight, enc_bias, dec_weight, dec_bias, first_moment, second_moment):
    feat = sizes[0]
    parts = sizes[1] * sizes[2]
    local = activations.shape[0]
    me = place(PARTS, sizes[1:]).astype(jnp.int32).reshape(1)
    near = swap(activations, "feat", feat, 1)
    mine, bias = widen(activations, dec_bias.reshape(1, -1))
    near, mine = lax.optimization_barrier((near, mine))
    pair = join(mine, near)
    rows = [pair] + [swap(pair, "feat", feat, k) for k in (2, 4, 6)]
    w3, w1 = fetch((3, 1), me, enc_weight, pair, parts)
    all_rows, x = center(rows, bias)
    x, w3, w1 = lax.optimization_barrier((x, w3, w1))
    p3, w2 = encode(me, x, w3, enc_weight, ahead=2)
    p1, w0 = encode(me, x, w1, enc_weight, ahead=0)
    p2 = encode(me, x, w2)
    arrived = [swap(p, PARTS, parts, k) for k, p in ((1, p1), (2, p2), (3, p3))]
    x, arrived[2] = lax.optimization_barrier((x, arrived[2]))
    p0 = encode(me, x, w0)
    arrived = [p0] + arrived

    w = pltpu.with_memory_space_constraint(dec_weight, pltpu.VMEM)
    sums = squares(w, p0)
    arrived, sums = lax.optimization_barrier((arrived, sums))
    act = activate(me, enc_bias.reshape(1, -1), arrived)
    act, sums = lax.optimization_barrier((act, sums))
    acts = [act] + [swap(act, PARTS, parts, k) for k in range(1, parts)]
    more = swap(sums, PARTS, parts, 1)
    part = rebuild_one(0, me, act, w)
    part = rebuild_one(EARLY, me, acts[EARLY], w, part)
    part, more = lax.optimization_barrier((part, more))
    sums = add(sums, more)
    acts, sums = lax.optimization_barrier((acts, sums))
    rest = [k for k in range(1, parts) if k != EARLY]
    part, all_act, counts = rebuild(rest, me, part, acts, w)
    part, narrow = pair_sum(part, swap(part, "feat", feat, 1))
    others = [swap(narrow, "feat", feat, k) for k in (2, 4, 6)]
    sums = (sums, swap(sums, PARTS, parts, 2))
    first = fill(2 * TALL, first_moment, second_moment, narrow)
    return adam(
        all_rows, part, others, bias, all_act, counts, sums, w, first, first_moment,
        second_moment, local,
    )


def plain(activations, enc_weight, enc_bias, dec_weight, dec_bias, first_moment, second_moment):
    local_rows = activations.shape[0]
    total_rows = local_rows * lax.axis_size("feat")
    centered = (activations.astype(f32) - dec_bias).astype(bf16)
    partial_value = jnp.dot(
        lax.all_gather(centered, "feat", axis=0, tiled=True), enc_weight, preferred_element_type=f32
    )
    wide = dec_weight.astype(f32)
    squares_sum = jnp.sum(wide * wide, axis=1)
    pre_sum, sum_squares = lax.psum((partial_value, squares_sum), PARTS)
    active = jnp.maximum(pre_sum + enc_bias, 0.0).astype(bf16)
    part = jnp.dot(active, dec_weight, preferred_element_type=f32)
    rebuilt = lax.psum_scatter(part, "feat", scatter_dimension=0, tiled=True) + dec_bias
    residual = (rebuilt - activations.astype(f32)).astype(bf16)
    all_residual = lax.all_gather(residual, "feat", axis=0, tiled=True)
    product = lax.dot_general(
        active, all_residual, (((0,), (0,)), ((), ())), preferred_element_type=f32
    )
    counts = jnp.sum(active.astype(f32), axis=0)
    row_norm = jnp.sqrt(sum_squares + norm_eps)
    gradient = (
        2.0 / total_rows * product
        + sparsity_coef / total_rows * counts[:, None] * wide / row_norm[:, None]
    )
    moment_one = beta_one * first_moment.astype(f32) + (1.0 - beta_one) * gradient
    moment_two = beta_two * second_moment.astype(f32) + (1.0 - beta_two) * gradient * gradient
    dec_step = moment_one / bias_one / (jnp.sqrt(moment_two / bias_two) + adam_eps)
    return rebuilt.astype(bf16), dec_step.astype(bf16)


def solution(mesh):
    sizes = tuple(mesh.shape[name] for name in ("feat", "row", "rep"))

    def shards(*args):
        local, depth = args[0].shape
        width = args[1].shape[1]
        fits = sizes[0] == 8 and local == 4 and depth % 128 == 0
        if fits and width % (TALL * sizes[1] * sizes[2]) == 0 and sizes[1] * sizes[2] == 4:
            return fast(sizes, *args)
        return plain(*args)

    split = P("feat", PARTS)
    return jax.shard_map(
        shards,
        mesh=mesh,
        in_specs=(split, P(PARTS, "feat"), P("feat"), split, P(PARTS), split, split),
        out_specs=(split, split),
        check_vma=False,
    )
```
